256 devices in a mesh: kvseq: 16 (over x, y_hi, core), kvhead: 8 (over z), section: 2 (over y_lo).
Axes of the slice: x: 4, y: 4 (y_hi: 2, y_lo: 2; y = y_hi * 2 + y_lo), z: 8, core: 2. Of those that a mesh axis runs over, the one named last changes fastest.
Arguments:
- hidden_in: bfloat16 [2, 8, 16384], P(None, None, 'kvseq')
- lengths: int32 [8], replicated, may hold values from 1 to 16384, as said below
- norm_gain: bfloat16 [2, 16384], P('section', 'kvseq'), may hold values from 0.099609375 to 1.8984375
- w_query: bfloat16 [2, 16384, 16384], P('section', 'kvseq', 'kvhead')
- w_keyval: bfloat16 [2, 16384, 8, 256], P('section', 'kvseq', 'kvhead')
- w_out: bfloat16 [2, 16384, 16384], P('section', 'kvhead', 'kvseq'), may hold values from -0.1875 to 0.1875
- kv_cache: bfloat16 [2, 8, 8, 16384, 256], P('section', 'kvhead', None, 'kvseq')
Outputs:
- layer_out: bfloat16 [2, 2, 8, 16384], P('section', None, None, 'kvseq')
The draws below stay inside these ranges and needn't reach their ends.
Inputs may be any that keep to these rules, and one draw needn't show every extreme that they name: `lengths`: some row has length 16384.
All inputs are finite; a program needn't handle non-finite values.
Results may differ from the reference program's by a relative error of at most 0.017.
Values may be sent and summed in bfloat16 or wider, within the bound.
No kernel may reach another device: no remote copies, remote signals or barrier semaphores. Data moves between devices by JAX's collectives and lax.ppermute only.
A program may use at most 64 MiB of HBM per device.

```python
import math
import jax
import jax.numpy as jnp
from jax import lax

D = 16384
GROUP = 16
HEAD_DIM = 128
ROWS = 8
CACHE_DEV = 1024
STEPS = 2
KVHEADS = 8
HEADS = 128
CTX = 16384
N_KVSEQ = 16
N_SECTION = 2


def shared_basis(key):
    return jax.random.normal(key, (N_SECTION, D, KVHEADS, 1, HEAD_DIM), jnp.float32) / math.sqrt(D)


def draw_w_query(key, part):
    basis = shared_basis(key)
    key = jax.random.fold_in(key, 14)
    shape_all = (N_SECTION, D, KVHEADS, GROUP, HEAD_DIM)
    noise = jax.random.normal(key, shape_all, jnp.float32) / math.sqrt(D)
    return ((basis + noise) * math.sqrt(0.5)).reshape(N_SECTION, D, HEADS * HEAD_DIM).astype(jnp.bfloat16)


def draw_w_keyval(key, part):
    basis = shared_basis(key)[:, :, :, 0, :]
    key = jax.random.fold_in(key, 15)
    key_key, value_key = jax.random.split(key)
    shape_half = (N_SECTION, D, KVHEADS, HEAD_DIM)
    key_noise = jax.random.normal(key_key, shape_half, jnp.float32) / math.sqrt(D)
    key_part = 1.1 * basis + key_noise
    value_part = jax.random.normal(value_key, shape_half, jnp.float32) / math.sqrt(D)
    return jnp.concatenate([key_part, value_part], axis=-1).astype(jnp.bfloat16)


def draw_lengths(key, part):
    key = jax.random.fold_in(key, 11)
    first_key, second_key = jax.random.split(key)
    drawn_lengths = jax.random.randint(first_key, (ROWS,), 1, CTX + 1)
    longest = jax.random.randint(second_key, (), 0, ROWS)
    return jnp.where(jnp.arange(ROWS) == longest, CTX, drawn_lengths).astype(jnp.int32)


def draw_hidden_in(key, part):
    key = jax.random.fold_in(key, 12)
    base_key, row_key, column_key = jax.random.split(key, 3)
    base_draw = jnp.clip(jax.random.normal(base_key, (STEPS, ROWS, D), jnp.float32), -3.0, 3.0)
    row_scale = jnp.exp(jax.random.uniform(row_key, (STEPS, ROWS, 1), jnp.float32, math.log(0.15), math.log(1.5)))
    column_scale = jnp.exp(jax.random.uniform(column_key, (1, 1, D), jnp.float32, math.log(0.3), math.log(3.0)))
    return (base_draw * row_scale * column_scale).astype(jnp.bfloat16)


def draw_kv_cache(key, part):
    key = jax.random.fold_in(key, 13)
    base_key = jax.random.fold_in(key, 0)
    shape_all = (N_SECTION, KVHEADS, ROWS, CTX, 2 * HEAD_DIM)
    channel = jnp.arange(2 * HEAD_DIM)
    channel_scale = jnp.where(channel < HEAD_DIM, 1.5, 1.0)
    base_draw = jnp.clip(jax.random.normal(base_key, shape_all, jnp.float32), -4.0, 4.0)
    return (base_draw * channel_scale).astype(jnp.bfloat16)


def block_levels(stream_key, dims, cuts, least, top_value):
    level, own = 1.0, jax.random.fold_in(stream_key, 6)
    for dim, parts in cuts:
        heights = jnp.exp(jax.random.uniform(jax.random.fold_in(own, dim), (parts,), jnp.float32, least / len(cuts), top_value / len(cuts)))
        level = level * jnp.repeat(heights, dims[dim] // parts).reshape([-1 if axis == dim else 1 for axis in range(len(dims))])
    return level


def gaussian(rng, extent, deviation, most, cuts=(), kind=jnp.bfloat16):
    loudness = block_levels(rng, extent, cuts, -0.22, 0.18) if cuts else 1.0
    array = jax.random.normal(rng, extent, jnp.float32) * deviation * loudness
    return jnp.minimum(jnp.maximum(array, -most), most).astype(kind)


def setup_inputs(seed: int = 0) -> dict:
    seeds = jax.random.split(jax.random.key(seed), 8)
    return {
        "hidden_in": draw_hidden_in(jax.random.fold_in(seeds[7], 71), 0),
        "lengths": draw_lengths(jax.random.fold_in(seeds[7], 71), 0),
        "norm_gain": jnp.clip(1.0 + 0.18 * jax.random.normal(seeds[2], (N_SECTION, D), jnp.float32), 0.099609375, 1.8984375).astype(jnp.bfloat16),
        "w_query": draw_w_query(jax.random.fold_in(seeds[7], 71), 0),
        "w_keyval": draw_w_keyval(jax.random.fold_in(seeds[7], 71), 0),
        "w_out": gaussian(seeds[5], (N_SECTION, HEADS * HEAD_DIM, D), (HEADS * HEAD_DIM // 16) ** -0.5, 0.1875, ((0, 2), (1, 8), (2, 16))),
        "kv_cache": draw_kv_cache(jax.random.fold_in(seeds[7], 71), 0),
    }


NEG_FLOOR = -1e+30
EPSILON = 1e-05

def project_rows(hidden, gain_row, query_mat, keyval_mat):
    scaled = (hidden.astype(jnp.float32) * gain_row.astype(jnp.float32)).astype(jnp.bfloat16)
    squares = lax.optimization_barrier(jnp.sum(jnp.square(hidden.astype(jnp.float32)), axis=-1))
    inv_rms = lax.rsqrt(squares / D + EPSILON)
    query_raw = jnp.dot(scaled, query_mat, preferred_element_type=jnp.float32)
    keyval_raw = jnp.dot(scaled, keyval_mat.reshape(D, KVHEADS * 2 * HEAD_DIM), preferred_element_type=jnp.float32)
    queries = (query_raw * inv_rms[:, None] * HEAD_DIM ** (-0.5)).astype(jnp.bfloat16)
    keyvals = (keyval_raw * inv_rms[:, None]).astype(jnp.bfloat16)
    return (queries.reshape(ROWS, KVHEADS, GROUP, HEAD_DIM), keyvals.reshape(ROWS, KVHEADS, 2 * HEAD_DIM))

def attend_head(queries, cache_head, recent, lengths):
    query_f32 = queries.astype(jnp.float32)
    key_rows = cache_head[..., :HEAD_DIM].astype(jnp.float32)
    value_rows = cache_head[..., HEAD_DIM:].astype(jnp.float32)
    scores = jnp.einsum('rgd,rcd->rgc', query_f32, key_rows).reshape(ROWS, GROUP, N_KVSEQ, CACHE_DEV)
    position = jnp.arange(CTX, dtype=jnp.int32).reshape(N_KVSEQ, CACHE_DEV)
    in_range = position[None, None] < lengths[:, None, None, None]
    block_max = lax.optimization_barrier(jnp.max(jnp.where(in_range, scores, NEG_FLOOR), axis=-1))
    weights = jnp.where(in_range, jnp.exp(scores - block_max[..., None]), 0.0)
    block_total = lax.optimization_barrier(jnp.sum(weights, axis=-1))
    rounded = lax.optimization_barrier(weights.astype(jnp.bfloat16)).astype(jnp.float32)
    block_acc = jnp.einsum('rgbc,rbcd->rgbd', rounded, value_rows.reshape(ROWS, N_KVSEQ, CACHE_DEV, HEAD_DIM))
    new_keys = recent[..., :HEAD_DIM].astype(jnp.float32)
    new_vals = recent[..., HEAD_DIM:].astype(jnp.float32)
    new_scores = jnp.einsum('rgd,nrd->rgn', query_f32, new_keys)
    row_top = jnp.maximum(lax.optimization_barrier(jnp.max(block_max, axis=-1)), lax.optimization_barrier(jnp.max(new_scores, axis=-1)))
    block_scale = jnp.exp(block_max - row_top[..., None])
    new_weights = jnp.exp(new_scores - row_top[..., None])
    numerator = jnp.einsum('rgb,rgbd->rgd', block_scale, block_acc) + jnp.einsum('rgn,nrd->rgd', new_weights, new_vals)
    denominator = lax.optimization_barrier(jnp.sum(block_scale * block_total, axis=-1)) + lax.optimization_barrier(jnp.sum(new_weights, axis=-1))
    return (numerator / denominator[..., None]).astype(jnp.bfloat16)

def reference(hidden_in, lengths, norm_gain, w_query, w_keyval, w_out, kv_cache):
    current = [hidden_in[step_no] for step_no in range(STEPS)]
    layer_list = []
    for section_no in range(N_SECTION):
        stored = []
        produced = []
        for step_no in range(STEPS):
            queries, keyvals = project_rows(current[step_no], norm_gain[section_no], w_query[section_no], w_keyval[section_no])
            stored.append(keyvals)
            recent = jnp.stack(stored)
            head_list = []
            for head_no in range(KVHEADS):
                head_list.append(attend_head(queries[:, head_no], kv_cache[section_no, head_no], recent[:, :, head_no], lengths))
            attended = jnp.stack(head_list, axis=1).reshape(ROWS, HEADS * HEAD_DIM)
            projected = jnp.dot(attended, w_out[section_no], preferred_element_type=jnp.float32)
            produced.append((current[step_no].astype(jnp.float32) + projected).astype(jnp.bfloat16))
        layer_list.append(jnp.stack(produced))
        current = produced
    return jnp.stack(layer_list)
```

```python
import functools

import jax
import jax.numpy as jnp
from jax import lax
from jax.experimental import pallas as pl
from jax.experimental.pallas import tpu as pltpu
from jax.sharding import PartitionSpec as P

D = 16384
HEAD_DIM = 128
NEG_FLOOR = -1e30
EPSILON = 1e-05
F32 = jnp.float32
BF16 = jnp.bfloat16
VMEM = pl.BlockSpec(memory_space=pltpu.VMEM)
SMEM = pl.BlockSpec(memory_space=pltpu.SMEM)
HALF = 1024
WIDE = HALF + 2 * HEAD_DIM
ROWS = 16
STAT = 8


def kvseq_perm(value, move):
    pairs = []
    for source in range(16):
        x, y, core = move(source // 4, (source // 2) % 2, source % 2)
        pairs.append((source, (x % 4) * 4 + y * 2 + core))
    return lax.ppermute(value, "kvseq", pairs)


def other_core(value):
    return kvseq_perm(value, lambda x, y, c: (x, y, 1 - c))


def z_perm(value, even, odd):
    pairs = [(z, (z + (odd if z % 2 else even)) % 8) for z in range(8)]
    return lax.ppermute(value, "kvhead", pairs)


def z_section_perm(value, flip):
    pairs = [(z * 2 + s, (z ^ flip) * 2 + 1 - s) for z in range(8) for s in range(2)]
    return lax.ppermute(value, ("kvhead", "section"), pairs)


def over_chips(value, join):
    value = join(value, kvseq_perm(value, lambda x, y, c: (x ^ 1, y, c)))
    value = join(value, kvseq_perm(value, lambda x, y, c: (3 - x, y, c)))
    return join(value, kvseq_perm(value, lambda x, y, c: (x, 1 - y, c)))


def project_kernel(ids_ref, hidden_ref, gain_ref, query_ref, keyval_ref, out_ref):
    hidden = hidden_ref[...].astype(F32)
    scaled = (hidden * gain_ref[...].astype(F32)).astype(BF16)
    squares = jnp.sum(hidden * hidden, axis=-1, keepdims=True)
    core = ids_ref[1]
    for part in range(2):
        half = core if part == 0 else 1 - core
        columns = pl.ds(pl.multiple_of(half * HALF, HALF), HALF)
        out_ref[part, :, :HALF] = jnp.dot(scaled, query_ref[:, columns], preferred_element_type=F32)
        columns = pl.ds(pl.multiple_of(half * HEAD_DIM, HEAD_DIM), HEAD_DIM)
        out_ref[part, :, HALF : HALF + HEAD_DIM] = jnp.dot(
            scaled, keyval_ref[:, columns], preferred_element_type=F32
        )
        out_ref[part, :, HALF + HEAD_DIM :] = jnp.broadcast_to(squares, (ROWS, HEAD_DIM))


def attend_kernel(ids_ref, len_ref, own_ref, oth_ref, cache_ref, out_ref, q_s, acc_s, stat_s, kv_s):
    seq_id, core = ids_ref[0], ids_ref[1]
    for part, ref in enumerate((own_ref, oth_ref)):
        inv_rms = lax.rsqrt(ref[:, HALF + HEAD_DIM : HALF + HEAD_DIM + 1] / D + EPSILON)
        queries = ref[:, :HALF] * inv_rms * HEAD_DIM ** (-0.5)
        queries = queries.astype(BF16).astype(F32)
        for g in range(8):
            q_s[pl.ds((part * 8 + g) * ROWS, ROWS), :] = queries[:, g * HEAD_DIM : (g + 1) * HEAD_DIM]
        fresh = (ref[:, HALF : HALF + HEAD_DIM] * inv_rms).astype(BF16).astype(F32)
        kv_s[core if part == 0 else 1 - core] = fresh
    lane = lax.broadcasted_iota(jnp.int32, (32, HEAD_DIM), 1)
    position = seq_id * 1024 + lax.broadcasted_iota(jnp.int32, (32, 1024), 1)
    step = lax.broadcasted_iota(jnp.int32, (32, 1), 0) // 16
    holder = seq_id == 0
    for r in range(8):
        q32 = jnp.concatenate(
            [q_s[pl.ds(t * 8 + r, 16, stride=ROWS), :] for t in range(2)], axis=0
        )
        scores = lax.dot_general(
            q32.astype(BF16),
            cache_ref[r, :, :HEAD_DIM],
            (((1,), (1,)), ((), ())),
            preferred_element_type=F32,
        )
        valid = position < len_ref[r]
        top = jnp.max(jnp.where(valid, scores, NEG_FLOOR), axis=-1, keepdims=True)
        weights = jnp.where(valid, jnp.exp(scores - top), 0.0)
        total = jnp.sum(weights, axis=-1, keepdims=True)
        acc = jnp.dot(weights.astype(BF16), cache_ref[r, :, HEAD_DIM:], preferred_element_type=F32)
        fresh_scores = []
        new_top = top
        for s in range(2):
            key = kv_s[0, pl.ds(s * 8 + r, 1), :]
            score = jnp.sum(q32 * key, axis=-1, keepdims=True)
            seen = (step >= s) & holder
            score = jnp.where(seen, score, NEG_FLOOR)
            new_top = jnp.maximum(new_top, score)
            fresh_scores.append((seen, score))
        scale = jnp.exp(top - new_top)
        acc = acc * scale
        total = total * scale
        for s in range(2):
            seen, score = fresh_scores[s]
            weight = jnp.where(seen, jnp.exp(score - new_top), 0.0)
            acc = acc + weight * kv_s[1, pl.ds(s * 8 + r, 1), :]
            total = total + weight
        stats = jnp.where(lane == 0, new_top, jnp.where(lane == 1, total, 0.0))
        for t in range(2):
            acc_s[pl.ds(t * 8 + r, 16, stride=ROWS), :] = acc[t * 16 : (t + 1) * 16]
            stat_s[pl.ds(t * 8 + r, 16, stride=ROWS), :] = stats[t * 16 : (t + 1) * 16]
    for part in range(2):
        rows = pl.ds(part * 128, 128)
        out_ref[part, :HEAD_DIM, :] = acc_s[rows, :].T
        out_ref[part, HEAD_DIM:, :] = stat_s[rows, :].T[:STAT]


def output_kernel(ids_ref, own_ref, oth_ref, w_ref, out_ref):
    core = ids_ref[1]
    result = None
    for part, ref in enumerate((own_ref, oth_ref)):
        half = core if part == 0 else 1 - core
        attended = (ref[:HEAD_DIM, :] / ref[HEAD_DIM + 1 : HEAD_DIM + 2, :]).T.astype(BF16)
        attended = jnp.concatenate([attended[g * ROWS : (g + 1) * ROWS] for g in range(8)], axis=1)
        rows = pl.ds(pl.multiple_of(half * HALF, HALF), HALF)
        term = jnp.dot(attended, w_ref[rows, :], preferred_element_type=F32)
        result = term if result is None else result + term
    out_ref[...] = result


def merge(left, right):
    left_max, right_max = left[HEAD_DIM : HEAD_DIM + 1], right[HEAD_DIM : HEAD_DIM + 1]
    top = jnp.maximum(left_max, right_max)
    left_scale, right_scale = jnp.exp(left_max - top), jnp.exp(right_max - top)
    row = lax.broadcasted_iota(jnp.int32, left.shape, 0)
    return jnp.where(row == HEAD_DIM, top, left * left_scale + right * right_scale)


def in_vmem(value):
    return pltpu.with_memory_space_constraint(value, pltpu.VMEM)


def per_device(hidden_in, lengths, norm_gain, w_query, w_keyval, w_out, kv_cache):
    section_id = lax.axis_index("section")
    seq_id = lax.axis_index("kvseq")
    core = seq_id % 2
    ids = jnp.stack([seq_id, core]).astype(jnp.int32)
    width = hidden_in.shape[2]
    w_query, w_keyval = in_vmem(w_query[0]), in_vmem(w_keyval[0, :, 0, :])
    w_out, cache = in_vmem(w_out[0]), in_vmem(kv_cache[0, 0])
    params = pltpu.CompilerParams(vmem_limit_bytes=24 * 2**20)

    def partial_layer(hidden):
        halves = pl.pallas_call(
            project_kernel,
            out_shape=jax.ShapeDtypeStruct((2, ROWS, WIDE), F32),
            in_specs=[SMEM] + [VMEM] * 4,
            out_specs=VMEM,
            compiler_params=params,
            name="project",
        )(ids, hidden, norm_gain, w_query, w_keyval)
        own = halves[0] + other_core(halves[1])
        own = over_chips(own, lambda a, b: a + b)
        oth = other_core(own)
        parts = pl.pallas_call(
            attend_kernel,
            out_shape=jax.ShapeDtypeStruct((2, HEAD_DIM + STAT, HEAD_DIM), F32),
            in_specs=[SMEM, SMEM] + [VMEM] * 3,
            out_specs=VMEM,
            scratch_shapes=[
                pltpu.VMEM((256, HEAD_DIM), F32),
                pltpu.VMEM((256, HEAD_DIM), F32),
                pltpu.VMEM((256, HEAD_DIM), F32),
                pltpu.VMEM((2, ROWS, HEAD_DIM), F32),
            ],
            compiler_params=params,
            name="attend",
        )(ids, lengths, own, oth, cache)
        own = merge(parts[0], other_core(parts[1]))
        own = over_chips(own, merge)
        oth = other_core(own)
        return pl.pallas_call(
            output_kernel,
            out_shape=jax.ShapeDtypeStruct((ROWS, width), F32),
            in_specs=[SMEM] + [VMEM] * 3,
            out_specs=VMEM,
            compiler_params=params,
            name="output",
        )(ids, own, oth, w_out)

    def over_heads(pair):
        near, far, opposite = z_perm(pair, -1, 1), z_perm(pair, -2, 2), z_perm(pair, -3, 3)
        return (pair + opposite) + (near + far)

    hidden = hidden_in.reshape(ROWS, width)
    partial = partial_layer(hidden)
    pair = z_section_perm(partial, 0) + z_section_perm(partial, 1)
    hidden = (hidden.astype(F32) + over_heads(pair)).astype(BF16)
    first = lax.ppermute(hidden, "section", [(0, 1), (1, 0)])
    partial = partial_layer(hidden)
    pair = partial + lax.ppermute(partial, "kvhead", [(z, z ^ 1) for z in range(8)])
    second = (hidden.astype(F32) + over_heads(pair)).astype(BF16)
    result = jnp.where(section_id == 0, first, second)
    return result.reshape(hidden_in.shape)[None]


def solution(mesh):
    placed = (
        P(None, None, "kvseq"),
        P(),
        P("section", "kvseq"),
        P("section", "kvseq", "kvhead"),
        P("section", "kvseq", "kvhead", None),
        P("section", "kvhead", "kvseq"),
        P("section", "kvhead", None, "kvseq", None),
    )
    return jax.shard_map(
        per_device,
        mesh=mesh,
        in_specs=placed,
        out_specs=P("section", None, None, "kvseq"),
        check_vma=False,
    )
```

```python
import functools

import jax
import jax.numpy as jnp
from jax import lax
from jax.experimental import pallas as pl
from jax.experimental.pallas import tpu as pltpu
from jax.sharding import PartitionSpec as P

D = 16384
HEAD_DIM = 128
NEG_FLOOR = -1e30
EPSILON = 1e-05
F32 = jnp.float32
BF16 = jnp.bfloat16
VMEM = pl.BlockSpec(memory_space=pltpu.VMEM)
SMEM = pl.BlockSpec(memory_space=pltpu.SMEM)
HBM = pl.BlockSpec(memory_space=pltpu.HBM)
HALF = 1024
WIDE = HALF + 2 * HEAD_DIM
ROWS = 16
STAT = 8


def permute(value, move, active=None):
    pairs = []
    for source in range(256):
        seq, z, section = source // 16, (source // 2) % 8, source % 2
        x, y, core = seq // 4, (seq // 2) % 2, seq % 2
        if active is None or section == active:
            x, y, core, z, section = move(x, y, core, z, section)
        else:
            core = 1 - core
        pairs.append((source, (x * 4 + y * 2 + core) * 16 + (z % 8) * 2 + section))
    return lax.ppermute(value, ("kvseq", "kvhead", "section"), pairs)


def other_core(value):
    return permute(value, lambda x, y, c, z, s: (x, y, 1 - c, z, s))


def over_chips(value, join, active):
    value = join(value, permute(value, lambda x, y, c, z, s: (3 - x, y, c, z, s), active))
    along_x = permute(value, lambda x, y, c, z, s: (x ^ 1, y, c, z, s), active)
    along_y = permute(value, lambda x, y, c, z, s: (x, 1 - y, c, z, s), active)
    along_both = permute(value, lambda x, y, c, z, s: (x ^ 1, 1 - y, c, z, s), active)
    return join(value, along_x, along_y, along_both)


def over_pairs(pair, active):
    def step(far):
        return permute(
            pair, lambda x, y, c, z, s: (x, y, c, z + (-far if z % 2 else far), s), active
        )

    return add(pair, step(3), step(1), step(2))


def add(left, *others):
    if len(others) == 1:
        return left + others[0]
    return (left + others[0]) + (others[1] + others[2])


def scale_rows(hidden, gain):
    hidden = hidden.astype(F32)
    scaled = (hidden * gain.astype(F32)).astype(BF16)
    return scaled, jnp.sum(hidden * hidden, axis=-1, keepdims=True)


def fetch_project_kernel(
    ids_ref, hidden_hbm, gain_hbm, query_hbm, keyval_hbm, first_out, second_out,
    hidden_ref, gain_ref, query_ref, keyval_ref, sems,
):
    core = ids_ref[1]
    chunk = HALF // 2
    copies = [
        pltpu.make_async_copy(hidden_hbm, hidden_ref, sems.at[0]),
        pltpu.make_async_copy(gain_hbm, gain_ref, sems.at[1]),
        pltpu.make_async_copy(keyval_hbm, keyval_ref, sems.at[2]),
    ]
    for part in range(4):
        half = 1 - core if part < 2 else core
        start = pl.multiple_of(half * HALF + part % 2 * chunk, chunk)
        copies.append(
            pltpu.make_async_copy(
                query_hbm.at[:, pl.ds(start, chunk)], query_ref.at[part], sems.at[3 + part]
            )
        )
    for copy in copies:
        copy.start()
    copies[0].wait()
    copies[1].wait()
    scaled, squares = scale_rows(hidden_ref[...], gain_ref[...])
    copies[2].wait()
    for half, out_ref in ((1 - core, first_out), (core, second_out)):
        out_ref[:, HALF + HEAD_DIM :] = jnp.broadcast_to(squares, (ROWS, HEAD_DIM))
        columns = pl.ds(pl.multiple_of(half * HEAD_DIM, HEAD_DIM), HEAD_DIM)
        out_ref[:, HALF : HALF + HEAD_DIM] = jnp.dot(
            scaled, keyval_ref[:, columns], preferred_element_type=F32
        )
    for part in range(4):
        copies[3 + part].wait()
        out_ref = first_out if part < 2 else second_out
        columns = slice(part % 2 * chunk, (part % 2 + 1) * chunk)
        out_ref[:, columns] = jnp.dot(scaled, query_ref[part], preferred_element_type=F32)


def project_half(half, scaled, query_ref, keyval_ref, out_ref):
    columns = pl.ds(pl.multiple_of(half * HALF, HALF), HALF)
    out_ref[:, :HALF] = jnp.dot(scaled, query_ref[:, columns], preferred_element_type=F32)
    columns = pl.ds(pl.multiple_of(half * HEAD_DIM, HEAD_DIM), HEAD_DIM)
    out_ref[:, HALF : HALF + HEAD_DIM] = jnp.dot(
        scaled, keyval_ref[:, columns], preferred_element_type=F32
    )


def project_kernel(ids_ref, hidden_ref, gain_ref, query_ref, keyval_ref, out_ref, scaled_ref):
    scaled, squares = scale_rows(hidden_ref[...], gain_ref[...])
    scaled_ref[...] = scaled
    out_ref[:, HALF + HEAD_DIM :] = jnp.broadcast_to(squares, (ROWS, HEAD_DIM))
    project_half(1 - ids_ref[1], scaled, query_ref, keyval_ref, out_ref)


def project_own_kernel(ids_ref, scaled_ref, first_ref, query_ref, keyval_ref, out_ref):
    out_ref[:, HALF + HEAD_DIM :] = first_ref[:, HALF + HEAD_DIM :]
    project_half(ids_ref[1], scaled_ref[...], query_ref, keyval_ref, out_ref)


def attend_kernel(
    ids_ref, len_ref, own_ref, oth_ref, cache_ref, first_out, second_out,
    q_s, kv_s, score_s, weight_s, acc_s, stat_s,
):
    seq_id, core = ids_ref[0], ids_ref[1]
    for part, ref in enumerate((own_ref, oth_ref)):
        inv_rms = lax.rsqrt(ref[:, HALF + HEAD_DIM : HALF + HEAD_DIM + 1] / D + EPSILON)
        queries = (ref[:, :HALF] * inv_rms * HEAD_DIM ** (-0.5)).astype(BF16).astype(F32)
        for g in range(8):
            q_s[pl.ds((part * 8 + g) * ROWS, ROWS), :] = queries[:, g * HEAD_DIM : (g + 1) * HEAD_DIM]
        fresh = (ref[:, HALF : HALF + HEAD_DIM] * inv_rms).astype(BF16).astype(F32)
        kv_s[core if part == 0 else 1 - core] = fresh
    for r in range(8):
        queries = q_s[pl.ds(r, 32, stride=8), :].astype(BF16)
        score_s[r] = lax.dot_general(
            queries,
            cache_ref[r, :, :HEAD_DIM],
            (((1,), (1,)), ((), ())),
            preferred_element_type=F32,
        )
    lane = lax.broadcasted_iota(jnp.int32, (32, HEAD_DIM), 1)
    position = seq_id * 1024 + lax.broadcasted_iota(jnp.int32, (32, 1024), 1)
    for r in range(8):
        scores = score_s[r]
        valid = position < len_ref[r]
        top = jnp.max(jnp.where(valid, scores, NEG_FLOOR), axis=-1, keepdims=True)
        weights = jnp.where(valid, jnp.exp(scores - top), 0.0)
        weight_s[r] = weights.astype(BF16)
        total = jnp.sum(weights, axis=-1, keepdims=True)
        stat_s[pl.ds(r, 32, stride=8), :] = jnp.where(lane == 0, top, total)
    for r in range(8):
        acc_s[pl.ds(r, 32, stride=8), :] = jnp.dot(
            weight_s[r], cache_ref[r, :, HEAD_DIM:], preferred_element_type=F32
        )
    row = lax.broadcasted_iota(jnp.int32, (HEAD_DIM, 1), 0)
    late = (row // 8) % 2 == 1
    holder = seq_id == 0
    lane = lax.broadcasted_iota(jnp.int32, (HEAD_DIM, HEAD_DIM), 1)
    for part, out_ref in enumerate((first_out, second_out)):
        rows = pl.ds(part * HEAD_DIM, HEAD_DIM)
        queries = q_s[rows, :]
        top, total, acc = stat_s[rows, 0:1], stat_s[rows, 1:2], acc_s[rows, :]
        new_top, fresh = top, []
        for t in range(2):
            key = jnp.concatenate([kv_s[0, pl.ds(t * 8, 8), :]] * 16, axis=0)
            score = jnp.sum(queries * key, axis=-1, keepdims=True)
            seen = (late & holder) if t else (row >= 0) & holder
            fresh.append((seen, score))
            new_top = jnp.maximum(new_top, jnp.where(seen, score, NEG_FLOOR))
        scale = jnp.exp(top - new_top)
        acc, total = acc * scale, total * scale
        for t, (seen, score) in enumerate(fresh):
            weight = jnp.where(seen, jnp.exp(score - new_top), 0.0)
            acc = acc + weight * jnp.concatenate([kv_s[1, pl.ds(t * 8, 8), :]] * 16, axis=0)
            total = total + weight
        out_ref[:HEAD_DIM, :] = acc.T
        out_ref[HEAD_DIM:, :] = jnp.where(lane == 0, new_top, total).T[:STAT]


def output_half(half, ref, w_ref):
    attended = (ref[:HEAD_DIM, :] / ref[HEAD_DIM + 1 : HEAD_DIM + 2, :]).T.astype(BF16)
    attended = jnp.concatenate([attended[g * ROWS : (g + 1) * ROWS] for g in range(8)], axis=1)
    rows = pl.ds(pl.multiple_of(half * HALF, HALF), HALF)
    return jnp.dot(attended, w_ref[rows, :], preferred_element_type=F32)


def output_own_kernel(ids_ref, own_ref, w_ref, out_ref):
    out_ref[...] = output_half(ids_ref[1], own_ref, w_ref)


def output_kernel(ids_ref, term_ref, oth_ref, w_ref, out_ref):
    out_ref[...] = term_ref[...] + output_half(1 - ids_ref[1], oth_ref, w_ref)


def merge(*parts):
    tops = [part[HEAD_DIM : HEAD_DIM + 1] for part in parts]
    top = functools.reduce(jnp.maximum, tops)
    scaled = [part * jnp.exp(own - top) for part, own in zip(parts, tops)]
    row = lax.broadcasted_iota(jnp.int32, parts[0].shape, 0)
    return jnp.where(row == HEAD_DIM, top, add(*scaled))


def in_hbm(value):
    return pltpu.with_memory_space_constraint(value, pltpu.HBM)


def in_vmem(value):
    return pltpu.with_memory_space_constraint(value, pltpu.VMEM)


def per_device(hidden_in, lengths, norm_gain, w_query, w_keyval, w_out, kv_cache):
    section_id = lax.axis_index("section")
    seq_id = lax.axis_index("kvseq")
    core = seq_id % 2
    ids = jnp.stack([seq_id, core]).astype(jnp.int32)
    width = hidden_in.shape[2]
    raw_query, raw_keyval = w_query[0], w_keyval[0, :, 0, :]
    w_query, w_keyval = in_vmem(raw_query), in_vmem(raw_keyval)
    w_out, cache = in_vmem(w_out[0]), in_vmem(kv_cache[0, 0])
    payload = jax.ShapeDtypeStruct((ROWS, WIDE), F32)
    part_shape = jax.ShapeDtypeStruct((HEAD_DIM + STAT, HEAD_DIM), F32)
    row_shape = jax.ShapeDtypeStruct((ROWS, width), F32)
    scaled_shape = jax.ShapeDtypeStruct((ROWS, width), BF16)

    def call(kernel, name, out_shape, in_specs, *args, scratch=()):
        return pl.pallas_call(
            kernel,
            out_shape=out_shape,
            in_specs=in_specs,
            out_specs=jax.tree.map(lambda _: VMEM, out_shape),
            scratch_shapes=scratch,
            compiler_params=pltpu.CompilerParams(vmem_limit_bytes=24 * 2**20),
            name=name,
        )(*args)

    def rest_of_layer(mine, oth, cache, active, extra=None):
        own = over_chips(mine + other_core(oth), add, active)
        if extra is not None:
            own, extra = lax.optimization_barrier((own, extra))
            extra = lax.ppermute(extra, "section", [(0, 1), (1, 0)])
        mine, oth = call(
            attend_kernel, "attend", (part_shape, part_shape), [SMEM, SMEM] + [VMEM] * 3,
            ids, lengths, own, other_core(own), cache,
            scratch=[
                pltpu.VMEM((256, HEAD_DIM), F32),
                pltpu.VMEM((2, ROWS, HEAD_DIM), F32),
                pltpu.VMEM((8, 32, 1024), F32),
                pltpu.VMEM((8, 32, 1024), BF16),
                pltpu.VMEM((256, HEAD_DIM), F32),
                pltpu.VMEM((256, HEAD_DIM), F32),
            ],
        )
        if extra is not None:
            oth, extra = lax.optimization_barrier((oth, extra))
        own = over_chips(merge(mine, other_core(oth)), merge, active)
        oth = other_core(own)
        term = call(
            output_own_kernel, "output_own", row_shape, [SMEM] + [VMEM] * 2, ids, own, w_out
        )
        partial = call(
            output_kernel, "output", row_shape, [SMEM] + [VMEM] * 3, ids, term, oth, w_out
        )
        return partial, extra

    hidden = hidden_in.reshape(ROWS, width)
    oth, mine = call(
        fetch_project_kernel, "project_first", (payload, payload), [SMEM] + [HBM] * 4,
        ids, in_hbm(hidden), in_hbm(norm_gain), in_hbm(raw_query), in_hbm(raw_keyval),
        scratch=[
            pltpu.VMEM((ROWS, width), BF16),
            pltpu.VMEM((1, width), BF16),
            pltpu.VMEM((4, width, HALF // 2), BF16),
            pltpu.VMEM((width, 2 * HEAD_DIM), BF16),
            pltpu.SemaphoreType.DMA((7,)),
        ],
    )
    partial, _ = rest_of_layer(mine, oth, cache, 0)
    pair = permute(partial, lambda x, y, c, z, s: (x, y, c, z, 1 - s))
    pair = pair + permute(partial, lambda x, y, c, z, s: (x, y, c, z + (1 if z % 2 else -1), 1 - s))
    hidden = (hidden.astype(F32) + over_pairs(pair, 1)).astype(BF16)
    oth, scaled = call(
        project_kernel, "project", (payload, scaled_shape), [SMEM] + [VMEM] * 4,
        ids, hidden, norm_gain, w_query, w_keyval,
    )
    mine = call(
        project_own_kernel, "project_own", payload, [SMEM] + [VMEM] * 4,
        ids, scaled, oth, w_query, w_keyval,
    )
    partial, first = rest_of_layer(mine, oth, cache, 1, hidden)
    pair = partial + permute(partial, lambda x, y, c, z, s: (x, y, c, z + (1 if z % 2 else -1), s), 1)
    second = (hidden.astype(F32) + over_pairs(pair, 1)).astype(BF16)
    result = jnp.where(section_id == 0, first, second)
    return result.reshape(hidden_in.shape)[None]


def solution(mesh):
    placed = (
        P(None, None, "kvseq"),
        P(),
        P("section", "kvseq"),
        P("section", "kvseq", "kvhead"),
        P("section", "kvseq", "kvhead", None),
        P("section", "kvhead", "kvseq"),
        P("section", "kvhead", None, "kvseq", None),
    )
    return jax.shard_map(
        per_device,
        mesh=mesh,
        in_specs=placed,
        out_specs=P("section", None, None, "kvseq"),
        check_vma=False,
    )
```

```python
import functools

import jax
import jax.numpy as jnp
from jax import lax
from jax.experimental import pallas as pl
from jax.experimental.pallas import tpu as pltpu
from jax.sharding import PartitionSpec as P

D = 16384
HEAD_DIM = 128
NEG_FLOOR = -1e30
EPSILON = 1e-05
F32 = jnp.float32
BF16 = jnp.bfloat16
VMEM = pl.BlockSpec(memory_space=pltpu.VMEM)
SMEM = pl.BlockSpec(memory_space=pltpu.SMEM)
HBM = pl.BlockSpec(memory_space=pltpu.HBM)
HALF = 1024
WIDE = HALF + 2 * HEAD_DIM
ROWS = 16
FETCHES = 8
FETCH = 128
STAT = 8


def permute(value, move, active=None):
    pairs = []
    for source in range(256):
        seq, z, section = source // 16, (source // 2) % 8, source % 2
        x, y, core = seq // 4, (seq // 2) % 2, seq % 2
        if active is None or section == active:
            x, y, core, z, section = move(x, y, core, z, section)
        else:
            core = 1 - core
        pairs.append((source, (x * 4 + y * 2 + core) * 16 + (z % 8) * 2 + section))
    return lax.ppermute(value, ("kvseq", "kvhead", "section"), pairs)


def other_core(value):
    return permute(value, lambda x, y, c, z, s: (x, y, 1 - c, z, s))


def over_chips(value, join, active):
    value = join(value, permute(value, lambda x, y, c, z, s: (x, 1 - y, c, z, s), active))
    steps = [
        permute(value, lambda x, y, c, z, s, k=k: (x ^ k, y, c, z, s), active) for k in (1, 3, 2)
    ]
    return join(value, *steps)


def over_pairs(pair, active):
    def step(far):
        return permute(
            pair, lambda x, y, c, z, s: (x, y, c, z + (-far if z % 2 else far), s), active
        )

    near, next_near, far = step(1), step(2), step(3)
    return add(pair, far, near, next_near)


def add(left, *others):
    if len(others) == 1:
        return left + others[0]
    return (left + others[0]) + (others[1] + others[2])


def scale_rows(hidden, gain):
    hidden = hidden.astype(F32)
    scaled = (hidden * gain.astype(F32)).astype(BF16)
    return scaled, jnp.sum(hidden * hidden, axis=-1, keepdims=True)


def fetch_project_kernel(
    ids_ref, hidden_hbm, gain_hbm, query_hbm, keyval_hbm, first_out, second_out,
    hidden_ref, gain_ref, query_ref, keyval_ref, sems,
):
    core = ids_ref[1]
    copies = [
        pltpu.make_async_copy(hidden_hbm, hidden_ref, sems.at[0]),
        pltpu.make_async_copy(gain_hbm, gain_ref, sems.at[1]),
    ]
    for part in range(FETCHES):
        rows = pl.ds(part * FETCH, FETCH)
        copies.append(
            pltpu.make_async_copy(query_hbm.at[rows], query_ref.at[rows], sems.at[3 + part])
        )
    copies.append(pltpu.make_async_copy(keyval_hbm, keyval_ref, sems.at[2]))
    for copy in copies:
        copy.start()
    copies[0].wait()
    copies[1].wait()
    scaled, squares = scale_rows(hidden_ref[...], gain_ref[...])
    queries = None
    for part in range(FETCHES):
        copies[2 + part].wait()
        rows = slice(part * FETCH, (part + 1) * FETCH)
        term = jnp.dot(scaled[:, rows], query_ref[rows, :], preferred_element_type=F32)
        queries = term if queries is None else queries + term
    copies[-1].wait()
    keyvals = jnp.dot(scaled, keyval_ref[...], preferred_element_type=F32)
    for out_ref, low in ((first_out, core == 1), (second_out, core == 0)):
        out_ref[:, :HALF] = jnp.where(low, queries[:, :HALF], queries[:, HALF:])
        out_ref[:, HALF : HALF + HEAD_DIM] = jnp.where(
            low, keyvals[:, :HEAD_DIM], keyvals[:, HEAD_DIM:]
        )
        out_ref[:, HALF + HEAD_DIM :] = jnp.broadcast_to(squares, (ROWS, HEAD_DIM))


def project_half(half, scaled, query_ref, keyval_ref, out_ref):
    columns = pl.ds(pl.multiple_of(half * HALF, HALF), HALF)
    out_ref[:, :HALF] = jnp.dot(scaled, query_ref[:, columns], preferred_element_type=F32)
    columns = pl.ds(pl.multiple_of(half * HEAD_DIM, HEAD_DIM), HEAD_DIM)
    out_ref[:, HALF : HALF + HEAD_DIM] = jnp.dot(
        scaled, keyval_ref[:, columns], preferred_element_type=F32
    )


def project_kernel(ids_ref, hidden_ref, gain_ref, query_ref, keyval_ref, out_ref, scaled_ref):
    scaled, squares = scale_rows(hidden_ref[...], gain_ref[...])
    scaled_ref[...] = scaled
    out_ref[:, HALF + HEAD_DIM :] = jnp.broadcast_to(squares, (ROWS, HEAD_DIM))
    project_half(1 - ids_ref[1], scaled, query_ref, keyval_ref, out_ref)


def project_own_kernel(ids_ref, scaled_ref, first_ref, query_ref, keyval_ref, out_ref):
    out_ref[:, HALF + HEAD_DIM :] = first_ref[:, HALF + HEAD_DIM :]
    project_half(ids_ref[1], scaled_ref[...], query_ref, keyval_ref, out_ref)


def attend_kernel(
    ids_ref, len_ref, own_ref, oth_ref, cache_ref, first_out, second_out,
    q_s, kv_s, score_s, weight_s, acc_s, stat_s,
):
    seq_id, core = ids_ref[0], ids_ref[1]
    for part, ref in enumerate((own_ref, oth_ref)):
        inv_rms = lax.rsqrt(ref[:, HALF + HEAD_DIM : HALF + HEAD_DIM + 1] / D + EPSILON)
        queries = (ref[:, :HALF] * inv_rms * HEAD_DIM ** (-0.5)).astype(BF16).astype(F32)
        for g in range(8):
            q_s[pl.ds((part * 8 + g) * ROWS, ROWS), :] = queries[:, g * HEAD_DIM : (g + 1) * HEAD_DIM]
        fresh = (ref[:, HALF : HALF + HEAD_DIM] * inv_rms).astype(BF16).astype(F32)
        kv_s[core if part == 0 else 1 - core] = fresh
    for r in range(8):
        queries = q_s[pl.ds(r, 32, stride=8), :].astype(BF16)
        score_s[r] = lax.dot_general(
            queries,
            cache_ref[r, :, :HEAD_DIM],
            (((1,), (1,)), ((), ())),
            preferred_element_type=F32,
        )
    lane = lax.broadcasted_iota(jnp.int32, (32, HEAD_DIM), 1)
    position = seq_id * 1024 + lax.broadcasted_iota(jnp.int32, (32, 1024), 1)
    for r in range(8):
        scores = score_s[r]
        valid = position < len_ref[r]
        top = jnp.max(jnp.where(valid, scores, NEG_FLOOR), axis=-1, keepdims=True)
        weights = jnp.where(valid, jnp.exp(scores - top), 0.0)
        weight_s[r] = weights.astype(BF16)
        total = jnp.sum(weights, axis=-1, keepdims=True)
        stat_s[pl.ds(r, 32, stride=8), :] = jnp.where(lane == 0, top, total)
    for r in range(8):
        acc_s[pl.ds(r, 32, stride=8), :] = jnp.dot(
            weight_s[r], cache_ref[r, :, HEAD_DIM:], preferred_element_type=F32
        )
    row = lax.broadcasted_iota(jnp.int32, (HEAD_DIM, 1), 0)
    late = (row // 8) % 2 == 1
    holder = seq_id == 0
    lane = lax.broadcasted_iota(jnp.int32, (HEAD_DIM, HEAD_DIM), 1)
    for part, out_ref in enumerate((first_out, second_out)):
        rows = pl.ds(part * HEAD_DIM, HEAD_DIM)
        queries = q_s[rows, :]
        top, total, acc = stat_s[rows, 0:1], stat_s[rows, 1:2], acc_s[rows, :]
        new_top, fresh = top, []
        for t in range(2):
            key = jnp.concatenate([kv_s[0, pl.ds(t * 8, 8), :]] * 16, axis=0)
            score = jnp.sum(queries * key, axis=-1, keepdims=True)
            seen = (late & holder) if t else (row >= 0) & holder
            fresh.append((seen, score))
            new_top = jnp.maximum(new_top, jnp.where(seen, score, NEG_FLOOR))
        scale = jnp.exp(top - new_top)
        acc, total = acc * scale, total * scale
        for t, (seen, score) in enumerate(fresh):
            weight = jnp.where(seen, jnp.exp(score - new_top), 0.0)
            acc = acc + weight * jnp.concatenate([kv_s[1, pl.ds(t * 8, 8), :]] * 16, axis=0)
            total = total + weight
        out_ref[:HEAD_DIM, :] = acc.T
        out_ref[HEAD_DIM:, :] = jnp.where(lane == 0, new_top, total).T[:STAT]


def output_half(half, ref, w_ref):
    attended = (ref[:HEAD_DIM, :] / ref[HEAD_DIM + 1 : HEAD_DIM + 2, :]).T.astype(BF16)
    attended = jnp.concatenate([attended[g * ROWS : (g + 1) * ROWS] for g in range(8)], axis=1)
    rows = pl.ds(pl.multiple_of(half * HALF, HALF), HALF)
    return jnp.dot(attended, w_ref[rows, :], preferred_element_type=F32)


def output_own_kernel(ids_ref, own_ref, w_ref, out_ref):
    out_ref[...] = output_half(ids_ref[1], own_ref, w_ref)


def output_kernel(ids_ref, term_ref, oth_ref, w_ref, out_ref):
    out_ref[...] = term_ref[...] + output_half(1 - ids_ref[1], oth_ref, w_ref)


def merge(*parts):
    tops = [part[HEAD_DIM : HEAD_DIM + 1] for part in parts]
    top = functools.reduce(jnp.maximum, tops)
    scaled = [part * jnp.exp(own - top) for part, own in zip(parts, tops)]
    row = lax.broadcasted_iota(jnp.int32, parts[0].shape, 0)
    return jnp.where(row == HEAD_DIM, top, add(*scaled))


def in_hbm(value):
    return pltpu.with_memory_space_constraint(value, pltpu.HBM)


def in_vmem(value):
    return pltpu.with_memory_space_constraint(value, pltpu.VMEM)


def per_device(hidden_in, lengths, norm_gain, w_query, w_keyval, w_out, kv_cache):
    section_id = lax.axis_index("section")
    seq_id = lax.axis_index("kvseq")
    core = seq_id % 2
    ids = jnp.stack([seq_id, core]).astype(jnp.int32)
    width = hidden_in.shape[2]
    raw_query, raw_keyval = w_query[0], w_keyval[0, :, 0, :]
    w_query, w_keyval = in_vmem(raw_query), in_vmem(raw_keyval)
    w_out, cache = in_vmem(w_out[0]), in_vmem(kv_cache[0, 0])
    payload = jax.ShapeDtypeStruct((ROWS, WIDE), F32)
    part_shape = jax.ShapeDtypeStruct((HEAD_DIM + STAT, HEAD_DIM), F32)
    row_shape = jax.ShapeDtypeStruct((ROWS, width), F32)
    scaled_shape = jax.ShapeDtypeStruct((ROWS, width), BF16)

    def call(kernel, name, out_shape, in_specs, *args, scratch=()):
        return pl.pallas_call(
            kernel,
            out_shape=out_shape,
            in_specs=in_specs,
            out_specs=jax.tree.map(lambda _: VMEM, out_shape),
            scratch_shapes=scratch,
            compiler_params=pltpu.CompilerParams(vmem_limit_bytes=24 * 2**20),
            name=name,
        )(*args)

    def rest_of_layer(mine, oth, cache, active, extra=None):
        own = over_chips(mine + other_core(oth), add, active)
        if extra is not None:
            own, extra = lax.optimization_barrier((own, extra))
            extra = lax.ppermute(extra, "section", [(0, 1), (1, 0)])
        mine, oth = call(
            attend_kernel, "attend", (part_shape, part_shape), [SMEM, SMEM] + [VMEM] * 3,
            ids, lengths, own, other_core(own), cache,
            scratch=[
                pltpu.VMEM((256, HEAD_DIM), F32),
                pltpu.VMEM((2, ROWS, HEAD_DIM), F32),
                pltpu.VMEM((8, 32, 1024), F32),
                pltpu.VMEM((8, 32, 1024), BF16),
                pltpu.VMEM((256, HEAD_DIM), F32),
                pltpu.VMEM((256, HEAD_DIM), F32),
            ],
        )
        own = over_chips(merge(mine, other_core(oth)), merge, active)
        if extra is not None:
            own, extra = lax.optimization_barrier((own, extra))
        oth = other_core(own)
        term = call(
            output_own_kernel, "output_own", row_shape, [SMEM] + [VMEM] * 2, ids, own, w_out
        )
        partial = call(
            output_kernel, "output", row_shape, [SMEM] + [VMEM] * 3, ids, term, oth, w_out
        )
        return partial, extra

    hidden = hidden_in.reshape(ROWS, width)
    oth, mine = call(
        fetch_project_kernel, "project_first", (payload, payload), [SMEM] + [HBM] * 4,
        ids, in_hbm(hidden), in_hbm(norm_gain), in_hbm(raw_query), in_hbm(raw_keyval),
        scratch=[
            pltpu.VMEM((ROWS, width), BF16),
            pltpu.VMEM((1, width), BF16),
            pltpu.VMEM((width, 2 * HALF), BF16),
            pltpu.VMEM((width, 2 * HEAD_DIM), BF16),
            pltpu.SemaphoreType.DMA((3 + FETCHES,)),
        ],
    )
    partial, _ = rest_of_layer(mine, oth, cache, 0)
    pair = permute(partial, lambda x, y, c, z, s: (x, y, c, z, 1 - s))
    pair = pair + permute(partial, lambda x, y, c, z, s: (x, y, c, z + (1 if z % 2 else -1), 1 - s))
    hidden = (hidden.astype(F32) + over_pairs(pair, 1)).astype(BF16)
    oth, scaled = call(
        project_kernel, "project", (payload, scaled_shape), [SMEM] + [VMEM] * 4,
        ids, hidden, norm_gain, w_query, w_keyval,
    )
    mine = call(
        project_own_kernel, "project_own", payload, [SMEM] + [VMEM] * 4,
        ids, scaled, oth, w_query, w_keyval,
    )
    partial, first = rest_of_layer(mine, oth, cache, 1, hidden)
    pair = partial + permute(partial, lambda x, y, c, z, s: (x, y, c, z + (1 if z % 2 else -1), s), 1)
    second = (hidden.astype(F32) + over_pairs(pair, 1)).astype(BF16)
    result = jnp.where(section_id == 0, first, second)
    return result.reshape(hidden_in.shape)[None]


def solution(mesh):
    placed = (
        P(None, None, "kvseq"),
        P(),
        P("section", "kvseq"),
        P("section", "kvseq", "kvhead"),
        P("section", "kvseq", "kvhead", None),
        P("section", "kvhead", "kvseq"),
        P("section", "kvhead", None, "kvseq", None),
    )
    return jax.shard_map(
        per_device,
        mesh=mesh,
        in_specs=placed,
        out_specs=P("section", None, None, "kvseq"),
        check_vma=False,
    )
```

```python
import functools

import jax
import jax.numpy as jnp
from jax import lax
from jax.experimental import pallas as pl
from jax.experimental.pallas import tpu as pltpu
from jax.sharding import PartitionSpec as P

D = 16384
HEAD_DIM = 128
NEG_FLOOR = -1e30
EPSILON = 1e-05
F32 = jnp.float32
BF16 = jnp.bfloat16
VMEM = pl.BlockSpec(memory_space=pltpu.VMEM)
SMEM = pl.BlockSpec(memory_space=pltpu.SMEM)
HBM = pl.BlockSpec(memory_space=pltpu.HBM)
HALF = 1024
WIDE = HALF + 2 * HEAD_DIM
ROWS = 16
FETCHES = 8
FETCH = 128
STAT = 8


def permute(value, move, active=None):
    pairs = []
    for source in range(256):
        seq, z, section = source // 16, (source // 2) % 8, source % 2
        x, y, core = seq // 4, (seq // 2) % 2, seq % 2
        if active is None or section == active:
            x, y, core, z, section = move(x, y, core, z, section)
        else:
            core = 1 - core
        pairs.append((source, (x * 4 + y * 2 + core) * 16 + (z % 8) * 2 + section))
    return lax.ppermute(value, ("kvseq", "kvhead", "section"), pairs)


def other_core(value):
    return permute(value, lambda x, y, c, z, s: (x, y, 1 - c, z, s))


def over_chips(value, join, active):
    value = join(value, permute(value, lambda x, y, c, z, s: (x, 1 - y, c, z, s), active))
    steps = [
        permute(value, lambda x, y, c, z, s, k=k: (x ^ k, y, c, z, s), active) for k in (1, 3, 2)
    ]
    return join(value, *steps)


def over_pairs(pair, active):
    def step(far):
        return permute(
            pair, lambda x, y, c, z, s: (x, y, c, z + (-far if z % 2 else far), s), active
        )

    near, next_near, far = step(1), step(2), step(3)
    return add(pair, far, near, next_near)


def add(left, *others):
    if len(others) == 1:
        return left + others[0]
    return (left + others[0]) + (others[1] + others[2])


def scale_rows(hidden, gain):
    hidden = hidden.astype(F32)
    scaled = (hidden * gain.astype(F32)).astype(BF16)
    return scaled, jnp.sum(hidden * hidden, axis=-1, keepdims=True)


def fetch_project_kernel(
    ids_ref, hidden_hbm, gain_hbm, query_hbm, keyval_hbm, first_out, second_out,
    hidden_ref, gain_ref, query_ref, keyval_ref, sems,
):
    core = ids_ref[1]
    copies = [
        pltpu.make_async_copy(hidden_hbm, hidden_ref, sems.at[0]),
        pltpu.make_async_copy(gain_hbm, gain_ref, sems.at[1]),
    ]
    for part in range(FETCHES):
        rows = pl.ds(part * FETCH, FETCH)
        copies.append(
            pltpu.make_async_copy(query_hbm.at[rows], query_ref.at[rows], sems.at[3 + part])
        )
    copies.append(pltpu.make_async_copy(keyval_hbm, keyval_ref, sems.at[2]))
    for copy in copies:
        copy.start()
    copies[0].wait()
    copies[1].wait()
    scaled, squares = scale_rows(hidden_ref[...], gain_ref[...])
    queries = None
    for part in range(FETCHES):
        copies[2 + part].wait()
        rows = slice(part * FETCH, (part + 1) * FETCH)
        term = jnp.dot(scaled[:, rows], query_ref[rows, :], preferred_element_type=F32)
        queries = term if queries is None else queries + term
    copies[-1].wait()
    keyvals = jnp.dot(scaled, keyval_ref[...], preferred_element_type=F32)
    for out_ref, low in ((first_out, core == 1), (second_out, core == 0)):
        out_ref[:, :HALF] = jnp.where(low, queries[:, :HALF], queries[:, HALF:])
        out_ref[:, HALF : HALF + HEAD_DIM] = jnp.where(
            low, keyvals[:, :HEAD_DIM], keyvals[:, HEAD_DIM:]
        )
        out_ref[:, HALF + HEAD_DIM :] = jnp.broadcast_to(squares, (ROWS, HEAD_DIM))


def project_half(half, scaled, query_ref, keyval_ref, out_ref):
    columns = pl.ds(pl.multiple_of(half * HALF, HALF), HALF)
    out_ref[:, :HALF] = jnp.dot(scaled, query_ref[:, columns], preferred_element_type=F32)
    columns = pl.ds(pl.multiple_of(half * HEAD_DIM, HEAD_DIM), HEAD_DIM)
    out_ref[:, HALF : HALF + HEAD_DIM] = jnp.dot(
        scaled, keyval_ref[:, columns], preferred_element_type=F32
    )


def project_kernel(ids_ref, hidden_ref, gain_ref, query_ref, keyval_ref, out_ref, scaled_ref):
    scaled, squares = scale_rows(hidden_ref[...], gain_ref[...])
    scaled_ref[...] = scaled
    out_ref[:, HALF + HEAD_DIM :] = jnp.broadcast_to(squares, (ROWS, HEAD_DIM))
    project_half(1 - ids_ref[1], scaled, query_ref, keyval_ref, out_ref)


def project_own_kernel(ids_ref, scaled_ref, first_ref, query_ref, keyval_ref, out_ref):
    out_ref[:, HALF + HEAD_DIM :] = first_ref[:, HALF + HEAD_DIM :]
    project_half(ids_ref[1], scaled_ref[...], query_ref, keyval_ref, out_ref)


def attend_kernel(
    ids_ref, len_ref, own_ref, oth_ref, cache_ref, first_out, second_out,
    q_s, kv_s, score_s, weight_s, acc_s, stat_s,
):
    seq_id, core = ids_ref[0], ids_ref[1]
    for part, ref in enumerate((own_ref, oth_ref)):
        inv_rms = lax.rsqrt(ref[:, HALF + HEAD_DIM : HALF + HEAD_DIM + 1] / D + EPSILON)
        queries = (ref[:, :HALF] * inv_rms * HEAD_DIM ** (-0.5)).astype(BF16).astype(F32)
        for g in range(8):
            q_s[pl.ds((part * 8 + g) * ROWS, ROWS), :] = queries[:, g * HEAD_DIM : (g + 1) * HEAD_DIM]
        fresh = (ref[:, HALF : HALF + HEAD_DIM] * inv_rms).astype(BF16).astype(F32)
        kv_s[core if part == 0 else 1 - core] = fresh
    for r in range(8):
        queries = q_s[pl.ds(r, 32, stride=8), :].astype(BF16)
        score_s[r] = lax.dot_general(
            queries,
            cache_ref[r, :, :HEAD_DIM],
            (((1,), (1,)), ((), ())),
            preferred_element_type=F32,
        )
    lane = lax.broadcasted_iota(jnp.int32, (32, HEAD_DIM), 1)
    position = seq_id * 1024 + lax.broadcasted_iota(jnp.int32, (32, 1024), 1)
    for r in range(8):
        scores = score_s[r]
        valid = position < len_ref[r]
        top = jnp.max(jnp.where(valid, scores, NEG_FLOOR), axis=-1, keepdims=True)
        weights = jnp.where(valid, jnp.exp(scores - top), 0.0)
        weight_s[r] = weights.astype(BF16)
        total = jnp.sum(weights, axis=-1, keepdims=True)
        stat_s[pl.ds(r, 32, stride=8), :] = jnp.where(lane == 0, top, total)
    for r in range(8):
        acc_s[pl.ds(r, 32, stride=8), :] = jnp.dot(
            weight_s[r], cache_ref[r, :, HEAD_DIM:], preferred_element_type=F32
        )
    row = lax.broadcasted_iota(jnp.int32, (HEAD_DIM, 1), 0)
    late = (row // 8) % 2 == 1
    holder = seq_id == 0
    lane = lax.broadcasted_iota(jnp.int32, (HEAD_DIM, HEAD_DIM), 1)
    for part, out_ref in enumerate((first_out, second_out)):
        rows = pl.ds(part * HEAD_DIM, HEAD_DIM)
        queries = q_s[rows, :]
        top, total, acc = stat_s[rows, 0:1], stat_s[rows, 1:2], acc_s[rows, :]
        new_top, fresh = top, []
        for t in range(2):
            key = jnp.concatenate([kv_s[0, pl.ds(t * 8, 8), :]] * 16, axis=0)
            score = jnp.sum(queries * key, axis=-1, keepdims=True)
            seen = (late & holder) if t else (row >= 0) & holder
            fresh.append((seen, score))
            new_top = jnp.maximum(new_top, jnp.where(seen, score, NEG_FLOOR))
        scale = jnp.exp(top - new_top)
        acc, total = acc * scale, total * scale
        for t, (seen, score) in enumerate(fresh):
            weight = jnp.where(seen, jnp.exp(score - new_top), 0.0)
            acc = acc + weight * jnp.concatenate([kv_s[1, pl.ds(t * 8, 8), :]] * 16, axis=0)
            total = total + weight
        out_ref[:HEAD_DIM, :] = acc.T
        out_ref[HEAD_DIM:, :] = jnp.where(lane == 0, new_top, total).T[:STAT]


def output_half(half, ref, w_ref):
    attended = (ref[:HEAD_DIM, :] / ref[HEAD_DIM + 1 : HEAD_DIM + 2, :]).T.astype(BF16)
    attended = jnp.concatenate([attended[g * ROWS : (g + 1) * ROWS] for g in range(8)], axis=1)
    rows = pl.ds(pl.multiple_of(half * HALF, HALF), HALF)
    return jnp.dot(attended, w_ref[rows, :], preferred_element_type=F32)


def output_own_kernel(ids_ref, own_ref, w_ref, out_ref):
    out_ref[...] = output_half(ids_ref[1], own_ref, w_ref)


def output_kernel(ids_ref, term_ref, oth_ref, w_ref, out_ref):
    out_ref[...] = term_ref[...] + output_half(1 - ids_ref[1], oth_ref, w_ref)


def add_kernel(left_ref, right_ref, out_ref):
    out_ref[...] = left_ref[...] + right_ref[...]


def merge(*parts):
    tops = [part[HEAD_DIM : HEAD_DIM + 1] for part in parts]
    top = functools.reduce(jnp.maximum, tops)
    scaled = [part * jnp.exp(own - top) for part, own in zip(parts, tops)]
    row = lax.broadcasted_iota(jnp.int32, parts[0].shape, 0)
    return jnp.where(row == HEAD_DIM, top, add(*scaled))


def in_hbm(value):
    return pltpu.with_memory_space_constraint(value, pltpu.HBM)


def in_vmem(value):
    return pltpu.with_memory_space_constraint(value, pltpu.VMEM)


def per_device(hidden_in, lengths, norm_gain, w_query, w_keyval, w_out, kv_cache):
    section_id = lax.axis_index("section")
    seq_id = lax.axis_index("kvseq")
    core = seq_id % 2
    ids = jnp.stack([seq_id, core]).astype(jnp.int32)
    width = hidden_in.shape[2]
    raw_query, raw_keyval = w_query[0], w_keyval[0, :, 0, :]
    w_query, w_keyval = in_vmem(raw_query), in_vmem(raw_keyval)
    w_out, cache = in_vmem(w_out[0]), in_vmem(kv_cache[0, 0])
    payload = jax.ShapeDtypeStruct((ROWS, WIDE), F32)
    part_shape = jax.ShapeDtypeStruct((HEAD_DIM + STAT, HEAD_DIM), F32)
    row_shape = jax.ShapeDtypeStruct((ROWS, width), F32)
    scaled_shape = jax.ShapeDtypeStruct((ROWS, width), BF16)

    def call(kernel, name, out_shape, in_specs, *args, scratch=(), cost=None):
        return pl.pallas_call(
            kernel,
            out_shape=out_shape,
            in_specs=in_specs,
            out_specs=jax.tree.map(lambda _: VMEM, out_shape),
            scratch_shapes=scratch,
            compiler_params=pltpu.CompilerParams(vmem_limit_bytes=24 * 2**20),
            cost_estimate=cost,
            name=name,
        )(*args)

    def rest_of_layer(own, cache, active, extra=None):
        own = over_chips(own, add, active)
        if extra is not None:
            own, extra = lax.optimization_barrier((own, extra))
            extra = lax.ppermute(extra, "section", [(0, 1), (1, 0)])
        mine, oth = call(
            attend_kernel, "attend", (part_shape, part_shape), [SMEM, SMEM] + [VMEM] * 3,
            ids, lengths, own, other_core(own), cache,
            scratch=[
                pltpu.VMEM((256, HEAD_DIM), F32),
                pltpu.VMEM((2, ROWS, HEAD_DIM), F32),
                pltpu.VMEM((8, 32, 1024), F32),
                pltpu.VMEM((8, 32, 1024), BF16),
                pltpu.VMEM((256, HEAD_DIM), F32),
                pltpu.VMEM((256, HEAD_DIM), F32),
            ],
        )
        own = over_chips(merge(mine, other_core(oth)), merge, active)
        if extra is not None:
            own, extra = lax.optimization_barrier((own, extra))
        oth = other_core(own)
        term = call(
            output_own_kernel, "output_own", row_shape, [SMEM] + [VMEM] * 2, ids, own, w_out
        )
        partial = call(
            output_kernel, "output", row_shape, [SMEM] + [VMEM] * 3, ids, term, oth, w_out
        )
        return partial, extra

    hidden = hidden_in.reshape(ROWS, width)
    oth, mine = call(
        fetch_project_kernel, "project_first", (payload, payload), [SMEM] + [HBM] * 4,
        ids, in_hbm(hidden), in_hbm(norm_gain), in_hbm(raw_query), in_hbm(raw_keyval),
        scratch=[
            pltpu.VMEM((ROWS, width), BF16),
            pltpu.VMEM((1, width), BF16),
            pltpu.VMEM((width, 2 * HALF), BF16),
            pltpu.VMEM((width, 2 * HEAD_DIM), BF16),
            pltpu.SemaphoreType.DMA((3 + FETCHES,)),
        ],
    )
    own = call(
        add_kernel, "add_first", payload, [VMEM, VMEM], mine, other_core(oth),
        cost=pl.CostEstimate(flops=2 * 10**10, bytes_accessed=10**8, transcendentals=0),
    )
    partial, _ = rest_of_layer(own, cache, 0)
    pair = permute(partial, lambda x, y, c, z, s: (x, y, c, z, 1 - s))
    pair = pair + permute(partial, lambda x, y, c, z, s: (x, y, c, z + (1 if z % 2 else -1), 1 - s))
    hidden = (hidden.astype(F32) + over_pairs(pair, 1)).astype(BF16)
    oth, scaled = call(
        project_kernel, "project", (payload, scaled_shape), [SMEM] + [VMEM] * 4,
        ids, hidden, norm_gain, w_query, w_keyval,
    )
    mine = call(
        project_own_kernel, "project_own", payload, [SMEM] + [VMEM] * 4,
        ids, scaled, oth, w_query, w_keyval,
    )
    partial, first = rest_of_layer(mine + other_core(oth), cache, 1, hidden)
    pair = partial + permute(partial, lambda x, y, c, z, s: (x, y, c, z + (1 if z % 2 else -1), s), 1)
    second = (hidden.astype(F32) + over_pairs(pair, 1)).astype(BF16)
    result = jnp.where(section_id == 0, first, second)
    return result.reshape(hidden_in.shape)[None]


def solution(mesh):
    placed = (
        P(None, None, "kvseq"),
        P(),
        P("section", "kvseq"),
        P("section", "kvseq", "kvhead"),
        P("section", "kvseq", "kvhead", None),
        P("section", "kvhead", "kvseq"),
        P("section", "kvhead", None, "kvseq", None),
    )
    return jax.shard_map(
        per_device,
        mesh=mesh,
        in_specs=placed,
        out_specs=P("section", None, None, "kvseq"),
        check_vma=False,
    )
```

```python
import functools

import jax
import jax.numpy as jnp
from jax import lax
from jax.experimental import pallas as pl
from jax.experimental.pallas import tpu as pltpu
from jax.sharding import PartitionSpec as P

D = 16384
HEAD_DIM = 128
NEG_FLOOR = -1e30
EPSILON = 1e-05
F32 = jnp.float32
BF16 = jnp.bfloat16
VMEM = pl.BlockSpec(memory_space=pltpu.VMEM)
SMEM = pl.BlockSpec(memory_space=pltpu.SMEM)
HBM = pl.BlockSpec(memory_space=pltpu.HBM)
HALF = 1024
WIDE = HALF + 2 * HEAD_DIM
ROWS = 16
FETCHES = 8
FETCH = 128
STAT = 8


def permute(value, move, active=None):
    pairs = []
    for source in range(256):
        seq, z, section = source // 16, (source // 2) % 8, source % 2
        x, y, core = seq // 4, (seq // 2) % 2, seq % 2
        if active is None or section == active:
            x, y, core, z, section = move(x, y, core, z, section)
        else:
            core = 1 - core
        pairs.append((source, (x * 4 + y * 2 + core) * 16 + (z % 8) * 2 + section))
    return lax.ppermute(value, ("kvseq", "kvhead", "section"), pairs)


def other_core(value):
    return permute(value, lambda x, y, c, z, s: (x, y, 1 - c, z, s))


def over_chips(value, join, active):
    value = join(value, permute(value, lambda x, y, c, z, s: (x, 1 - y, c, z, s), active))
    steps = [
        permute(value, lambda x, y, c, z, s, k=k: (x ^ k, y, c, z, s), active) for k in (1, 3, 2)
    ]
    return join(value, *steps)


def over_pairs(pair, active):
    def step(far):
        return permute(
            pair, lambda x, y, c, z, s: (x, y, c, z + (-far if z % 2 else far), s), active
        )

    near, next_near, far = step(1), step(2), step(3)
    return add(pair, far, near, next_near)


def add(left, *others):
    if len(others) == 1:
        return left + others[0]
    return (left + others[0]) + (others[1] + others[2])


def scale_rows(hidden, gain):
    hidden = hidden.astype(F32)
    scaled = (hidden * gain.astype(F32)).astype(BF16)
    return scaled, jnp.sum(hidden * hidden, axis=-1, keepdims=True)


def fetch_project_kernel(
    ids_ref, hidden_hbm, gain_hbm, query_hbm, keyval_hbm, first_out, second_out,
    hidden_ref, gain_ref, query_ref, keyval_ref, sems,
):
    core = ids_ref[1]
    copies = [
        pltpu.make_async_copy(hidden_hbm, hidden_ref, sems.at[0]),
        pltpu.make_async_copy(gain_hbm, gain_ref, sems.at[1]),
    ]
    for part in range(FETCHES):
        rows = pl.ds(part * FETCH, FETCH)
        copies.append(
            pltpu.make_async_copy(query_hbm.at[rows], query_ref.at[rows], sems.at[3 + part])
        )
    copies.append(pltpu.make_async_copy(keyval_hbm, keyval_ref, sems.at[2]))
    for copy in copies:
        copy.start()
    copies[0].wait()
    copies[1].wait()
    scaled, squares = scale_rows(hidden_ref[...], gain_ref[...])
    queries = None
    for part in range(FETCHES):
        copies[2 + part].wait()
        rows = slice(part * FETCH, (part + 1) * FETCH)
        term = jnp.dot(scaled[:, rows], query_ref[rows, :], preferred_element_type=F32)
        queries = term if queries is None else queries + term
    copies[-1].wait()
    keyvals = jnp.dot(scaled, keyval_ref[...], preferred_element_type=F32)
    for out_ref, low in ((first_out, core == 1), (second_out, core == 0)):
        out_ref[:, :HALF] = jnp.where(low, queries[:, :HALF], queries[:, HALF:])
        out_ref[:, HALF : HALF + HEAD_DIM] = jnp.where(
            low, keyvals[:, :HEAD_DIM], keyvals[:, HEAD_DIM:]
        )
        out_ref[:, HALF + HEAD_DIM :] = jnp.broadcast_to(squares, (ROWS, HEAD_DIM))


def project_half(half, scaled, query_ref, keyval_ref, out_ref):
    columns = pl.ds(pl.multiple_of(half * HALF, HALF), HALF)
    out_ref[:, :HALF] = jnp.dot(scaled, query_ref[:, columns], preferred_element_type=F32)
    columns = pl.ds(pl.multiple_of(half * HEAD_DIM, HEAD_DIM), HEAD_DIM)
    out_ref[:, HALF : HALF + HEAD_DIM] = jnp.dot(
        scaled, keyval_ref[:, columns], preferred_element_type=F32
    )


def project_kernel(ids_ref, hidden_ref, gain_ref, query_ref, keyval_ref, out_ref, scaled_ref):
    scaled, squares = scale_rows(hidden_ref[...], gain_ref[...])
    scaled_ref[...] = scaled
    out_ref[:, HALF + HEAD_DIM :] = jnp.broadcast_to(squares, (ROWS, HEAD_DIM))
    project_half(1 - ids_ref[1], scaled, query_ref, keyval_ref, out_ref)


def project_own_kernel(ids_ref, scaled_ref, first_ref, query_ref, keyval_ref, out_ref):
    out_ref[:, HALF + HEAD_DIM :] = first_ref[:, HALF + HEAD_DIM :]
    project_half(ids_ref[1], scaled_ref[...], query_ref, keyval_ref, out_ref)


def attend_kernel(
    ids_ref, len_ref, own_ref, oth_ref, cache_ref, first_out, second_out,
    q_s, kv_s, score_s, weight_s, acc_s, stat_s,
):
    seq_id, core = ids_ref[0], ids_ref[1]
    for part, ref in enumerate((own_ref, oth_ref)):
        inv_rms = lax.rsqrt(ref[:, HALF + HEAD_DIM : HALF + HEAD_DIM + 1] / D + EPSILON)
        queries = (ref[:, :HALF] * inv_rms * HEAD_DIM ** (-0.5)).astype(BF16).astype(F32)
        for g in range(8):
            q_s[pl.ds((part * 8 + g) * ROWS, ROWS), :] = queries[:, g * HEAD_DIM : (g + 1) * HEAD_DIM]
        fresh = (ref[:, HALF : HALF + HEAD_DIM] * inv_rms).astype(BF16).astype(F32)
        kv_s[core if part == 0 else 1 - core] = fresh
    for r in range(8):
        queries = q_s[pl.ds(r, 32, stride=8), :].astype(BF16)
        score_s[r] = lax.dot_general(
            queries,
            cache_ref[r, :, :HEAD_DIM],
            (((1,), (1,)), ((), ())),
            preferred_element_type=F32,
        )
    lane = lax.broadcasted_iota(jnp.int32, (32, HEAD_DIM), 1)
    position = seq_id * 1024 + lax.broadcasted_iota(jnp.int32, (32, 1024), 1)
    for r in range(8):
        scores = score_s[r]
        valid = position < len_ref[r]
        top = jnp.max(jnp.where(valid, scores, NEG_FLOOR), axis=-1, keepdims=True)
        weights = jnp.where(valid, jnp.exp(scores - top), 0.0)
        weight_s[r] = weights.astype(BF16)
        total = jnp.sum(weights, axis=-1, keepdims=True)
        stat_s[pl.ds(r, 32, stride=8), :] = jnp.where(lane == 0, top, total)
    for r in range(8):
        acc_s[pl.ds(r, 32, stride=8), :] = jnp.dot(
            weight_s[r], cache_ref[r, :, HEAD_DIM:], preferred_element_type=F32
        )
    row = lax.broadcasted_iota(jnp.int32, (HEAD_DIM, 1), 0)
    late = (row // 8) % 2 == 1
    holder = seq_id == 0
    lane = lax.broadcasted_iota(jnp.int32, (HEAD_DIM, HEAD_DIM), 1)
    for part, out_ref in enumerate((first_out, second_out)):
        rows = pl.ds(part * HEAD_DIM, HEAD_DIM)
        queries = q_s[rows, :]
        top, total, acc = stat_s[rows, 0:1], stat_s[rows, 1:2], acc_s[rows, :]
        new_top, fresh = top, []
        for t in range(2):
            key = jnp.concatenate([kv_s[0, pl.ds(t * 8, 8), :]] * 16, axis=0)
            score = jnp.sum(queries * key, axis=-1, keepdims=True)
            seen = (late & holder) if t else (row >= 0) & holder
            fresh.append((seen, score))
            new_top = jnp.maximum(new_top, jnp.where(seen, score, NEG_FLOOR))
        scale = jnp.exp(top - new_top)
        acc, total = acc * scale, total * scale
        for t, (seen, score) in enumerate(fresh):
            weight = jnp.where(seen, jnp.exp(score - new_top), 0.0)
            acc = acc + weight * jnp.concatenate([kv_s[1, pl.ds(t * 8, 8), :]] * 16, axis=0)
            total = total + weight
        out_ref[:HEAD_DIM, :] = acc.T
        out_ref[HEAD_DIM:, :] = jnp.where(lane == 0, new_top, total).T[:STAT]


def output_half(half, ref, w_ref):
    attended = (ref[:HEAD_DIM, :] / ref[HEAD_DIM + 1 : HEAD_DIM + 2, :]).T.astype(BF16)
    attended = jnp.concatenate([attended[g * ROWS : (g + 1) * ROWS] for g in range(8)], axis=1)
    rows = pl.ds(pl.multiple_of(half * HALF, HALF), HALF)
    return jnp.dot(attended, w_ref[rows, :], preferred_element_type=F32)


def output_own_kernel(ids_ref, own_ref, w_ref, out_ref):
    out_ref[...] = output_half(ids_ref[1], own_ref, w_ref)


def output_kernel(ids_ref, term_ref, oth_ref, w_ref, out_ref):
    out_ref[...] = term_ref[...] + output_half(1 - ids_ref[1], oth_ref, w_ref)


def add_kernel(left_ref, right_ref, out_ref):
    out_ref[...] = left_ref[...] + right_ref[...]


def merge(*parts):
    tops = [part[HEAD_DIM : HEAD_DIM + 1] for part in parts]
    top = functools.reduce(jnp.maximum, tops)
    scaled = [part * jnp.exp(own - top) for part, own in zip(parts, tops)]
    row = lax.broadcasted_iota(jnp.int32, parts[0].shape, 0)
    return jnp.where(row == HEAD_DIM, top, add(*scaled))


def in_hbm(value):
    return pltpu.with_memory_space_constraint(value, pltpu.HBM)


def in_vmem(value):
    return pltpu.with_memory_space_constraint(value, pltpu.VMEM)


def per_device(hidden_in, lengths, norm_gain, w_query, w_keyval, w_out, kv_cache):
    section_id = lax.axis_index("section")
    seq_id = lax.axis_index("kvseq")
    core = seq_id % 2
    ids = jnp.stack([seq_id, core]).astype(jnp.int32)
    width = hidden_in.shape[2]
    raw_query, raw_keyval = w_query[0], w_keyval[0, :, 0, :]
    w_query, w_keyval = in_vmem(raw_query), in_vmem(raw_keyval)
    w_out, cache = in_vmem(w_out[0]), in_vmem(kv_cache[0, 0])
    payload = jax.ShapeDtypeStruct((ROWS, WIDE), F32)
    part_shape = jax.ShapeDtypeStruct((HEAD_DIM + STAT, HEAD_DIM), F32)
    row_shape = jax.ShapeDtypeStruct((ROWS, width), F32)
    scaled_shape = jax.ShapeDtypeStruct((ROWS, width), BF16)

    def call(kernel, name, out_shape, in_specs, *args, scratch=(), cost=None):
        return pl.pallas_call(
            kernel,
            out_shape=out_shape,
            in_specs=in_specs,
            out_specs=jax.tree.map(lambda _: VMEM, out_shape),
            scratch_shapes=scratch,
            compiler_params=pltpu.CompilerParams(vmem_limit_bytes=24 * 2**20),
            cost_estimate=cost,
            name=name,
        )(*args)

    def rest_of_layer(own, cache, active, extra=None):
        own = over_chips(own, add, active)
        if extra is not None:
            own, extra = lax.optimization_barrier((own, extra))
            extra = lax.ppermute(extra, "section", [(0, 1), (1, 0)])
        mine, oth = call(
            attend_kernel, "attend", (part_shape, part_shape), [SMEM, SMEM] + [VMEM] * 3,
            ids, lengths, own, other_core(own), cache,
            scratch=[
                pltpu.VMEM((264, HEAD_DIM), F32),
                pltpu.VMEM((2, ROWS, HEAD_DIM), F32),
                pltpu.VMEM((8, 32, 1024), F32),
                pltpu.VMEM((8, 32, 1024), BF16),
                pltpu.VMEM((264, HEAD_DIM), F32),
                pltpu.VMEM((264, HEAD_DIM), F32),
            ],
        )
        own = over_chips(merge(mine, other_core(oth)), merge, active)
        if extra is not None:
            own, extra = lax.optimization_barrier((own, extra))
        oth = other_core(own)
        term = call(
            output_own_kernel, "output_own", row_shape, [SMEM] + [VMEM] * 2, ids, own, w_out
        )
        partial = call(
            output_kernel, "output", row_shape, [SMEM] + [VMEM] * 3, ids, term, oth, w_out
        )
        return partial, extra

    hidden = hidden_in.reshape(ROWS, width)
    oth, mine = call(
        fetch_project_kernel, "project_first", (payload, payload), [SMEM] + [HBM] * 4,
        ids, in_hbm(hidden), in_hbm(norm_gain), in_hbm(raw_query), in_hbm(raw_keyval),
        scratch=[
            pltpu.VMEM((ROWS, width), BF16),
            pltpu.VMEM((1, width), BF16),
            pltpu.VMEM((width, 2 * HALF), BF16),
            pltpu.VMEM((width, 2 * HEAD_DIM), BF16),
            pltpu.SemaphoreType.DMA((3 + FETCHES,)),
        ],
    )
    own = call(
        add_kernel, "add_first", payload, [VMEM, VMEM], mine, other_core(oth),
        cost=pl.CostEstimate(flops=2 * 10**10, bytes_accessed=10**8, transcendentals=0),
    )
    partial, _ = rest_of_layer(own, cache, 0)
    pair = permute(partial, lambda x, y, c, z, s: (x, y, c, z, 1 - s))
    pair = pair + permute(partial, lambda x, y, c, z, s: (x, y, c, z + (1 if z % 2 else -1), 1 - s))
    hidden = (hidden.astype(F32) + over_pairs(pair, 1)).astype(BF16)
    oth, scaled = call(
        project_kernel, "project", (payload, scaled_shape), [SMEM] + [VMEM] * 4,
        ids, hidden, norm_gain, w_query, w_keyval,
    )
    mine = call(
        project_own_kernel, "project_own", payload, [SMEM] + [VMEM] * 4,
        ids, scaled, oth, w_query, w_keyval,
    )
    partial, first = rest_of_layer(mine + other_core(oth), cache, 1, hidden)
    pair = partial + permute(partial, lambda x, y, c, z, s: (x, y, c, z + (1 if z % 2 else -1), s), 1)
    second = (hidden.astype(F32) + over_pairs(pair, 1)).astype(BF16)
    result = jnp.where(section_id == 0, first, second)
    return result.reshape(hidden_in.shape)[None]


def solution(mesh):
    placed = (
        P(None, None, "kvseq"),
        P(),
        P("section", "kvseq"),
        P("section", "kvseq", "kvhead"),
        P("section", "kvseq", "kvhead", None),
        P("section", "kvhead", "kvseq"),
        P("section", "kvhead", None, "kvseq", None),
    )
    return jax.shard_map(
        per_device,
        mesh=mesh,
        in_specs=placed,
        out_specs=P("section", None, None, "kvseq"),
        check_vma=False,
    )
```

```python
import functools

import jax
import jax.numpy as jnp
from jax import lax
from jax.experimental import pallas as pl
from jax.experimental.pallas import tpu as pltpu
from jax.sharding import PartitionSpec as P

D = 16384
HEAD_DIM = 128
NEG_FLOOR = -1e30
EPSILON = 1e-05
F32 = jnp.float32
BF16 = jnp.bfloat16
VMEM = pl.BlockSpec(memory_space=pltpu.VMEM)
SMEM = pl.BlockSpec(memory_space=pltpu.SMEM)
HBM = pl.BlockSpec(memory_space=pltpu.HBM)
HALF = 1024
WIDE = HALF + 3 * HEAD_DIM
SQUARES = HALF + 2 * HEAD_DIM
ROWS = 16
FETCHES = 8
FETCH = 128
STAT = 8


def permute(value, move, active=None):
    pairs = []
    for source in range(256):
        seq, z, section = source // 16, (source // 2) % 8, source % 2
        x, y, core = seq // 4, (seq // 2) % 2, seq % 2
        if active is None or section == active:
            x, y, core, z, section = move(x, y, core, z, section)
        else:
            core = 1 - core
        pairs.append((source, (x * 4 + y * 2 + core) * 16 + (z % 8) * 2 + section))
    return lax.ppermute(value, ("kvseq", "kvhead", "section"), pairs)


def other_core(value):
    return permute(value, lambda x, y, c, z, s: (x, y, 1 - c, z, s))


def over_chips(value, join, active):
    value = join(value, permute(value, lambda x, y, c, z, s: (x, 1 - y, c, z, s), active))
    steps = [
        permute(value, lambda x, y, c, z, s, k=k: (x ^ k, y, c, z, s), active) for k in (1, 3, 2)
    ]
    return join(value, *steps)


def over_pairs(pair, active):
    def step(far):
        return permute(
            pair, lambda x, y, c, z, s: (x, y, c, z + (-far if z % 2 else far), s), active
        )

    near, next_near, far = step(1), step(2), step(3)
    return add(pair, far, near, next_near)


def add(left, *others):
    if len(others) == 1:
        return left + others[0]
    return (left + others[0]) + (others[1] + others[2])


def scale_rows(hidden, gain):
    hidden = hidden.astype(F32)
    scaled = (hidden * gain.astype(F32)).astype(BF16)
    return scaled, jnp.sum(hidden * hidden, axis=-1, keepdims=True)


def fetch_project_kernel(
    ids_ref, hidden_hbm, gain_hbm, query_hbm, keyval_hbm, first_out, second_out,
    hidden_ref, gain_ref, query_ref, keyval_ref, sems,
):
    core = ids_ref[1]
    copies = [
        pltpu.make_async_copy(hidden_hbm, hidden_ref, sems.at[0]),
        pltpu.make_async_copy(gain_hbm, gain_ref, sems.at[1]),
    ]
    for part in range(FETCHES):
        rows = pl.ds(part * FETCH, FETCH)
        copies.append(
            pltpu.make_async_copy(query_hbm.at[rows], query_ref.at[rows], sems.at[3 + part])
        )
    copies.append(pltpu.make_async_copy(keyval_hbm, keyval_ref, sems.at[2]))
    for copy in copies:
        copy.start()
    copies[0].wait()
    copies[1].wait()
    scaled, squares = scale_rows(hidden_ref[...], gain_ref[...])
    queries = None
    for part in range(FETCHES):
        copies[2 + part].wait()
        rows = slice(part * FETCH, (part + 1) * FETCH)
        term = jnp.dot(scaled[:, rows], query_ref[rows, :], preferred_element_type=F32)
        queries = term if queries is None else queries + term
    copies[-1].wait()
    keyvals = jnp.dot(scaled, keyval_ref[...], preferred_element_type=F32)
    for out_ref, low in ((first_out, core == 1), (second_out, core == 0)):
        out_ref[:, :HALF] = jnp.where(low, queries[:, :HALF], queries[:, HALF:])
        out_ref[:, HALF:SQUARES] = keyvals
        out_ref[:, SQUARES:] = jnp.broadcast_to(squares, (ROWS, HEAD_DIM))


def project_half(half, scaled, query_ref, keyval_ref, out_ref):
    columns = pl.ds(pl.multiple_of(half * HALF, HALF), HALF)
    out_ref[:, :HALF] = jnp.dot(scaled, query_ref[:, columns], preferred_element_type=F32)
    out_ref[:, HALF:SQUARES] = jnp.dot(scaled, keyval_ref[...], preferred_element_type=F32)


def project_kernel(ids_ref, hidden_ref, gain_ref, query_ref, keyval_ref, out_ref, scaled_ref):
    scaled, squares = scale_rows(hidden_ref[...], gain_ref[...])
    scaled_ref[...] = scaled
    out_ref[:, SQUARES:] = jnp.broadcast_to(squares, (ROWS, HEAD_DIM))
    project_half(1 - ids_ref[1], scaled, query_ref, keyval_ref, out_ref)


def project_own_kernel(ids_ref, scaled_ref, first_ref, query_ref, keyval_ref, out_ref):
    out_ref[:, SQUARES:] = first_ref[:, SQUARES:]
    project_half(ids_ref[1], scaled_ref[...], query_ref, keyval_ref, out_ref)


def attend_kernel(
    ids_ref, len_ref, own_ref, cache_ref, sibling_ref, out_ref,
    q_s, kv_s, score_s, weight_s, acc_s, stat_s,
):
    seq_id = ids_ref[0]
    inv_rms = lax.rsqrt(own_ref[:, SQUARES : SQUARES + 1] / D + EPSILON)
    queries = (own_ref[:, :HALF] * inv_rms * HEAD_DIM ** (-0.5)).astype(BF16).astype(F32)
    for g in range(8):
        q_s[pl.ds(g * ROWS, ROWS), :] = queries[:, g * HEAD_DIM : (g + 1) * HEAD_DIM]
    for part in range(2):
        start = HALF + part * HEAD_DIM
        fresh = own_ref[:, start : start + HEAD_DIM] * inv_rms
        kv_s[part] = fresh.astype(BF16).astype(F32)
    blocks = (cache_ref, sibling_ref)
    for r in range(8):
        queries = q_s[pl.ds(r, 16, stride=8), :].astype(BF16)
        for part, block in enumerate(blocks):
            score_s[r, part * 16 : part * 16 + 16] = lax.dot_general(
                queries,
                block[r, :, :HEAD_DIM],
                (((1,), (1,)), ((), ())),
                preferred_element_type=F32,
            )
    lane = lax.broadcasted_iota(jnp.int32, (32, HEAD_DIM), 1)
    sibling_id = seq_id + 1 - 2 * ids_ref[1]
    in_own = lax.broadcasted_iota(jnp.int32, (32, 1024), 0) < 16
    position = lax.broadcasted_iota(jnp.int32, (32, 1024), 1)
    position = position + 1024 * jnp.where(in_own, seq_id, sibling_id)
    for r in range(8):
        scores = score_s[r]
        valid = position < len_ref[r]
        top = jnp.max(jnp.where(valid, scores, NEG_FLOOR), axis=-1, keepdims=True)
        weights = jnp.where(valid, jnp.exp(scores - top), 0.0)
        weight_s[r] = weights.astype(BF16)
        total = jnp.sum(weights, axis=-1, keepdims=True)
        stats = jnp.where(lane == 0, top, total)
        for part in range(2):
            stat_s[part, pl.ds(r, 16, stride=8), :] = stats[part * 16 : part * 16 + 16]
    for r in range(8):
        for part, block in enumerate(blocks):
            acc_s[part, pl.ds(r, 16, stride=8), :] = jnp.dot(
                weight_s[r, part * 16 : part * 16 + 16],
                block[r, :, HEAD_DIM:],
                preferred_element_type=F32,
            )
    rows = slice(0, HEAD_DIM)
    row = lax.broadcasted_iota(jnp.int32, (HEAD_DIM, 1), 0)
    late = (row // 8) % 2 == 1
    holder = seq_id < 2
    lane = lax.broadcasted_iota(jnp.int32, (HEAD_DIM, HEAD_DIM), 1)
    queries = q_s[rows, :]
    tops = [stat_s[part, rows, 0:1] for part in range(2)]
    new_top, found = jnp.maximum(tops[0], tops[1]), []
    for t in range(2):
        key = jnp.concatenate([kv_s[0, pl.ds(t * 8, 8), :]] * 16, axis=0)
        score = jnp.sum(queries * key, axis=-1, keepdims=True)
        seen = (late & holder) if t else (row >= 0) & holder
        found.append((seen, score))
        new_top = jnp.maximum(new_top, jnp.where(seen, score, NEG_FLOOR))
    scales = [jnp.exp(top - new_top) for top in tops]
    acc = acc_s[0, rows, :] * scales[0] + acc_s[1, rows, :] * scales[1]
    total = stat_s[0, rows, 1:2] * scales[0] + stat_s[1, rows, 1:2] * scales[1]
    for t, (seen, score) in enumerate(found):
        weight = jnp.where(seen, jnp.exp(score - new_top), 0.0)
        acc = acc + weight * jnp.concatenate([kv_s[1, pl.ds(t * 8, 8), :]] * 16, axis=0)
        total = total + weight
    out_ref[:HEAD_DIM, :] = acc.T
    out_ref[HEAD_DIM:, :] = jnp.where(lane == 0, new_top, total).T[:STAT]


def output_half(half, ref, w_ref):
    attended = (ref[:HEAD_DIM, :] / ref[HEAD_DIM + 1 : HEAD_DIM + 2, :]).T.astype(BF16)
    attended = jnp.concatenate([attended[g * ROWS : (g + 1) * ROWS] for g in range(8)], axis=1)
    rows = pl.ds(pl.multiple_of(half * HALF, HALF), HALF)
    return jnp.dot(attended, w_ref[rows, :], preferred_element_type=F32)


def output_own_kernel(ids_ref, own_ref, w_ref, out_ref):
    out_ref[...] = output_half(ids_ref[1], own_ref, w_ref)


def output_kernel(ids_ref, term_ref, oth_ref, w_ref, out_ref):
    out_ref[...] = term_ref[...] + output_half(1 - ids_ref[1], oth_ref, w_ref)


def add_kernel(left_ref, right_ref, out_ref):
    out_ref[...] = left_ref[...] + right_ref[...]


def merge(*parts):
    tops = [part[HEAD_DIM : HEAD_DIM + 1] for part in parts]
    top = functools.reduce(jnp.maximum, tops)
    scaled = [part * jnp.exp(own - top) for part, own in zip(parts, tops)]
    row = lax.broadcasted_iota(jnp.int32, parts[0].shape, 0)
    return jnp.where(row == HEAD_DIM, top, add(*scaled))


def in_hbm(value):
    return pltpu.with_memory_space_constraint(value, pltpu.HBM)


def in_vmem(value):
    return pltpu.with_memory_space_constraint(value, pltpu.VMEM)


def per_device(hidden_in, lengths, norm_gain, w_query, w_keyval, w_out, kv_cache):
    section_id = lax.axis_index("section")
    seq_id = lax.axis_index("kvseq")
    core = seq_id % 2
    ids = jnp.stack([seq_id, core]).astype(jnp.int32)
    width = hidden_in.shape[2]
    raw_query, raw_keyval = w_query[0], w_keyval[0, :, 0, :]
    w_query, w_keyval = in_vmem(raw_query), in_vmem(raw_keyval)
    w_out, cache = in_vmem(w_out[0]), in_vmem(kv_cache[0, 0])
    payload = jax.ShapeDtypeStruct((ROWS, WIDE), F32)
    part_shape = jax.ShapeDtypeStruct((HEAD_DIM + STAT, HEAD_DIM), F32)
    row_shape = jax.ShapeDtypeStruct((ROWS, width), F32)
    scaled_shape = jax.ShapeDtypeStruct((ROWS, width), BF16)

    def call(kernel, name, out_shape, in_specs, *args, scratch=(), cost=None):
        return pl.pallas_call(
            kernel,
            out_shape=out_shape,
            in_specs=in_specs,
            out_specs=jax.tree.map(lambda _: VMEM, out_shape),
            scratch_shapes=scratch,
            compiler_params=pltpu.CompilerParams(vmem_limit_bytes=24 * 2**20),
            cost_estimate=cost,
            name=name,
        )(*args)

    def rest_of_layer(own, sibling, active, extra=None):
        own = over_chips(own, add, active)
        if extra is not None:
            own, extra = lax.optimization_barrier((own, extra))
            extra = lax.ppermute(extra, "section", [(0, 1), (1, 0)])
        part = call(
            attend_kernel, "attend", part_shape, [SMEM, SMEM] + [VMEM] * 3,
            ids, lengths, own, cache, sibling,
            scratch=[
                pltpu.VMEM((136, HEAD_DIM), F32),
                pltpu.VMEM((2, ROWS, HEAD_DIM), F32),
                pltpu.VMEM((8, 32, 1024), F32),
                pltpu.VMEM((8, 32, 1024), BF16),
                pltpu.VMEM((2, 136, HEAD_DIM), F32),
                pltpu.VMEM((2, 136, HEAD_DIM), F32),
            ],
        )
        own = over_chips(part, merge, active)
        if extra is not None:
            own, extra = lax.optimization_barrier((own, extra))
        oth = other_core(own)
        term = call(
            output_own_kernel, "output_own", row_shape, [SMEM] + [VMEM] * 2, ids, own, w_out
        )
        partial = call(
            output_kernel, "output", row_shape, [SMEM] + [VMEM] * 3, ids, term, oth, w_out
        )
        return partial, extra

    hidden = hidden_in.reshape(ROWS, width)
    oth, mine = call(
        fetch_project_kernel, "project_first", (payload, payload), [SMEM] + [HBM] * 4,
        ids, in_hbm(hidden), in_hbm(norm_gain), in_hbm(raw_query), in_hbm(raw_keyval),
        scratch=[
            pltpu.VMEM((ROWS, width), BF16),
            pltpu.VMEM((1, width), BF16),
            pltpu.VMEM((width, 2 * HALF), BF16),
            pltpu.VMEM((width, 2 * HEAD_DIM), BF16),
            pltpu.SemaphoreType.DMA((3 + FETCHES,)),
        ],
    )
    own = call(
        add_kernel, "add_first", payload, [VMEM, VMEM], mine, other_core(oth),
        cost=pl.CostEstimate(flops=2 * 10**10, bytes_accessed=10**8, transcendentals=0),
    )
    raw_cache, own = lax.optimization_barrier((kv_cache[0, 0], own))
    sibling = in_vmem(other_core(raw_cache))
    partial, _ = rest_of_layer(own, sibling, 0)
    pair = permute(partial, lambda x, y, c, z, s: (x, y, c, z, 1 - s))
    pair = pair + permute(partial, lambda x, y, c, z, s: (x, y, c, z + (1 if z % 2 else -1), 1 - s))
    hidden = (hidden.astype(F32) + over_pairs(pair, 1)).astype(BF16)
    oth, scaled = call(
        project_kernel, "project", (payload, scaled_shape), [SMEM] + [VMEM] * 4,
        ids, hidden, norm_gain, w_query, w_keyval,
    )
    mine = call(
        project_own_kernel, "project_own", payload, [SMEM] + [VMEM] * 4,
        ids, scaled, oth, w_query, w_keyval,
    )
    partial, first = rest_of_layer(mine + other_core(oth), sibling, 1, hidden)
    pair = partial + permute(partial, lambda x, y, c, z, s: (x, y, c, z + (1 if z % 2 else -1), s), 1)
    second = (hidden.astype(F32) + over_pairs(pair, 1)).astype(BF16)
    result = jnp.where(section_id == 0, first, second)
    return result.reshape(hidden_in.shape)[None]


def solution(mesh):
    placed = (
        P(None, None, "kvseq"),
        P(),
        P("section", "kvseq"),
        P("section", "kvseq", "kvhead"),
        P("section", "kvseq", "kvhead", None),
        P("section", "kvhead", "kvseq"),
        P("section", "kvhead", None, "kvseq", None),
    )
    return jax.shard_map(
        per_device,
        mesh=mesh,
        in_specs=placed,
        out_specs=P("section", None, None, "kvseq"),
        check_vma=False,
    )
```
